32 devices in a mesh: teacher: 4 (over x, core), vocab: 8 (over z, y).
Axes of the slice: x: 2, y: 2, z: 4, core: 2. Of those that a mesh axis runs over, the one named last changes fastest.
Arguments:
- teacher_hidden: bfloat16 [4, 512, 4096], P('teacher', 'vocab'), may hold values from -28 to 28
- teacher_gain: float32 [4, 4096], P('teacher'), may hold values from 0.25 to 1.75
- teacher_head: bfloat16 [4, 4096, 77824], P('teacher', None, 'vocab'), may hold values from -2 to 2
- student_hidden: bfloat16 [512, 896], P(('teacher', 'vocab')), may hold values from -10 to 10
- student_head: bfloat16 [896, 77824], P(None, 'vocab'), may hold values from -2 to 2
- targets: int32 [512], P(('teacher', 'vocab')), may hold values from 0 to 77823
Outputs:
- row_loss: float32 [512], P(('teacher', 'vocab'))
- grad_hidden: bfloat16 [512, 896], P(('teacher', 'vocab'))
- grad_head: float32 [896, 77824], P('teacher', 'vocab')
The draws below stay inside these ranges and needn't reach their ends.
All inputs are finite; a program needn't handle non-finite values.
Results may differ from the reference program's by a relative error of at most 0.0098.
The reference program's roundings to bfloat16 on the way (of `normed` and `grad_logits`) count: a program that leaves them out, or rounds other values in their place, can miss the bound.
Values may be sent and summed in bfloat16 or wider, within the bound.
No kernel may reach another device: no remote copies, remote signals or barrier semaphores. Data moves between devices by JAX's collectives and lax.ppermute only.
A program may use at most 256 MiB of HBM per device.

```python
import math
import jax
import jax.numpy as jnp
from jax import lax

D = 4096
V = 77824
DS = 896
TOK = 512
TEACHERS = 4


def rough_values(key, shape):
    return jax.random.truncated_normal(key, -4.0, 4.0, shape, jnp.float32)


def draw_teacher_hidden(key, part):
    common = rough_values(jax.random.fold_in(key, 11), (1, TOK, D))
    individual = rough_values(jax.random.fold_in(key, 12), (TEACHERS, TOK, D))
    hidden = common + 0.6 * individual
    return hidden.astype(jnp.bfloat16)


def draw_teacher_head(key, part):
    col_factor = jnp.full((V,), 20.0 / math.sqrt(D), jnp.float32)
    common = rough_values(jax.random.fold_in(key, 21), (D, V))

    def one_teacher(teacher_index):
        individual = rough_values(jax.random.fold_in(jax.random.fold_in(key, 22), teacher_index), (D, V))
        matrix = (0.1 * common + individual) * col_factor[None, :]
        return matrix.astype(jnp.bfloat16)
    return lax.map(one_teacher, jnp.arange(TEACHERS))


def draw_student_hidden(key, part):
    hidden = rough_values(jax.random.fold_in(key, 31), (TOK, DS))
    return hidden.astype(jnp.bfloat16)


def draw_student_head(key, part):
    col_factor = jnp.full((V,), 2.7 / math.sqrt(DS), jnp.float32)
    matrix = rough_values(jax.random.fold_in(key, 41), (DS, V)) * col_factor[None, :]
    return matrix.astype(jnp.bfloat16)


def with_ends(array, own_key, low, high):
    index_at = [jax.random.randint(jax.random.fold_in(own_key, axis), (), 0, length) for axis, length in enumerate(array.shape)]
    main_axis = array.shape.index(max(array.shape))
    neighbour = index_at[:main_axis] + [(index_at[main_axis] + 1) % array.shape[main_axis]] + index_at[main_axis + 1:]
    return array.at[tuple(index_at)].set(low).at[tuple(neighbour)].set(high)


def setup_inputs(seed: int = 0) -> dict:
    key_list = jax.random.split(jax.random.key(seed), 7)
    return {
        "teacher_hidden": draw_teacher_hidden(jax.random.fold_in(key_list[6], 71), 0),
        "teacher_gain": jnp.clip(1.0 + 0.15 * jax.random.normal(key_list[1], (TEACHERS, D), jnp.float32), 0.25, 1.75),
        "teacher_head": draw_teacher_head(jax.random.fold_in(key_list[6], 71), 0),
        "student_hidden": draw_student_hidden(jax.random.fold_in(key_list[6], 71), 0),
        "student_head": draw_student_head(jax.random.fold_in(key_list[6], 71), 0),
        "targets": with_ends(jax.random.randint(key_list[5], (TOK,), 0, V), jax.random.fold_in(key_list[5], 1), 0, V - 1).astype(jnp.int32),
    }


EPSILON = 1e-06
LABEL_WEIGHT = 0.5

def log_softmax_rows(logits):
    row_peak = lax.optimization_barrier(jnp.max(logits, axis=1, keepdims=True))
    return logits - (row_peak + jnp.log(lax.optimization_barrier(jnp.sum(jnp.exp(logits - row_peak), axis=1, keepdims=True))))

def reference(teacher_hidden, teacher_gain, teacher_head, student_hidden, student_head, targets):
    weight = 1.0 / TEACHERS

    def add_teacher(running, inputs):
        hidden = inputs[0].astype(jnp.float32)
        gain_row = inputs[1]
        scale_rows = lax.rsqrt(lax.optimization_barrier(jnp.mean(hidden * hidden, axis=1, keepdims=True)) + EPSILON)
        normed = (hidden * scale_rows * gain_row[None, :]).astype(jnp.bfloat16)
        return (running + jnp.dot(normed, inputs[2], preferred_element_type=jnp.float32) * weight, None)
    mean_logits = lax.scan(add_teacher, jnp.zeros((TOK, V), jnp.float32), (teacher_hidden, teacher_gain, teacher_head))[0]
    log_target = log_softmax_rows(mean_logits)
    student_logits = jnp.dot(student_hidden, student_head, preferred_element_type=jnp.float32)
    log_student = log_softmax_rows(student_logits)
    target_prob = jnp.exp(log_target)
    student_prob = jnp.exp(log_student)
    columns = lax.broadcasted_iota(jnp.int32, (1, V), 1)
    is_target = targets[:, None] == columns
    row_loss = lax.optimization_barrier(jnp.sum(target_prob * (log_target - log_student), axis=1)) - LABEL_WEIGHT * lax.optimization_barrier(jnp.sum(jnp.where(is_target, log_student, 0.0), axis=1))
    grad_logits = ((1.0 + LABEL_WEIGHT) * student_prob - target_prob - LABEL_WEIGHT * is_target.astype(jnp.float32)).astype(jnp.bfloat16)
    grad_hidden = lax.dot_general(grad_logits, student_head, (((1,), (1,)), ((), ())), preferred_element_type=jnp.float32).astype(jnp.bfloat16)
    grad_head = lax.dot_general(student_hidden, grad_logits, (((0,), (0,)), ((), ())), preferred_element_type=jnp.float32)
    return (row_loss, grad_hidden, grad_head)
```

```python
import functools

import jax
import jax.numpy as jnp
from jax import lax
from jax.experimental import pallas as pl
from jax.experimental.pallas import tpu as pltpu
from jax.sharding import PartitionSpec as P

EPSILON = 1e-06
LABEL_WEIGHT = 0.5
VMEM_LIMIT = 48 * 2**20


def column_plan(columns, parts):
    tile = next((w for w in (512, 256, 128) if columns % w == 0), columns)
    tiles = columns // tile
    parts = min(parts, tiles)
    edges = [(tiles * k + parts - 1) // parts for k in range(parts + 1)]
    return tile, [(a, b - a) for a, b in zip(edges[:-1], edges[1:])]


def teacher_kernel(half, weight, x_ref, w_ref, sibling_ref, own_ref):
    sums = jnp.dot(x_ref[...], w_ref[0], preferred_element_type=jnp.float32) * weight
    sibling_ref[...] = sums[:half]
    own_ref[...] = sums[half:]


def teacher_chunk(x, head, weight, tile, first, count):
    rows, depth = x.shape
    half = rows // 2
    return pl.pallas_call(
        functools.partial(teacher_kernel, half, weight),
        grid=(count,),
        in_specs=[
            pl.BlockSpec((rows, depth), lambda i: (0, 0)),
            pl.BlockSpec((1, depth, tile), lambda i: (0, 0, i + first)),
        ],
        out_specs=[pl.BlockSpec((half, tile), lambda i: (0, i))] * 2,
        out_shape=[jax.ShapeDtypeStruct((half, tile * count), jnp.float32)] * 2,
        compiler_params=pltpu.CompilerParams(vmem_limit_bytes=VMEM_LIMIT),
        cost_estimate=pl.CostEstimate(
            flops=2 * rows * depth * tile * count,
            bytes_accessed=2 * depth * tile * count + 4 * rows * tile * count,
            transcendentals=0,
        ),
    )(x, head)


def head_grad_kernel(parts, *refs):
    h_refs, g_refs, out_ref = refs[:parts], refs[parts : 2 * parts], refs[-1]
    total = None
    for h_ref, g_ref in zip(h_refs, g_refs):
        term = jnp.dot(h_ref[...], g_ref[...], preferred_element_type=jnp.float32)
        total = term if total is None else total + term
    out_ref[...] = total


def head_grad_chunk(h_parts, g_parts, so_far, columns, tile, first, count):
    parts, features, rows = len(h_parts), h_parts[0].shape[0], h_parts[0].shape[1]
    in_specs = [pl.BlockSpec((features, rows), lambda i: (0, 0))] * parts
    in_specs += [pl.BlockSpec((rows, tile), lambda i: (0, i))] * parts
    operands = list(h_parts) + list(g_parts)
    alias = {}
    if so_far is not None:
        alias = {len(operands): 0}
        in_specs.append(pl.BlockSpec(memory_space=pl.ANY))
        operands.append(so_far)
    return pl.pallas_call(
        functools.partial(head_grad_kernel, parts),
        grid=(count,),
        in_specs=in_specs,
        out_specs=pl.BlockSpec((features, tile), lambda i: (0, i + first)),
        out_shape=jax.ShapeDtypeStruct((features, columns), jnp.float32),
        input_output_aliases=alias,
        compiler_params=pltpu.CompilerParams(vmem_limit_bytes=VMEM_LIMIT),
        cost_estimate=pl.CostEstimate(
            flops=2 * features * rows * parts * tile * count,
            bytes_accessed=(2 * rows * parts + 4 * features) * tile * count,
            transcendentals=0,
        ),
    )(*operands)


class Vocab:
    def __init__(self):
        self.n = lax.axis_size("vocab")
        self.me = lax.axis_index("vocab")
        self.ring = self.n // 2 if self.n in (4, 8) else 0

    def from_ahead(self, a, k):
        n = self.ring
        pairs = [(v, 2 * ((v // 2 - k) % n) + v % 2) for v in range(self.n)]
        return lax.ppermute(a, "vocab", pairs)

    def to_ahead(self, a, k):
        n = self.ring
        pairs = [(v, 2 * ((v // 2 + k) % n) + v % 2) for v in range(self.n)]
        return lax.ppermute(a, "vocab", pairs)

    def across(self, a):
        return lax.ppermute(a, "vocab", [(v, v ^ 1) for v in range(self.n)])

    def slot_of(self, v):
        if not self.ring:
            return v
        return 2 * ((v // 2 - self.me // 2) % self.ring) + ((v % 2) ^ (self.me % 2))

    def holder_of(self, slot):
        if not self.ring:
            return slot
        return 2 * ((slot // 2 + self.me // 2) % self.ring) + ((slot % 2) ^ (self.me % 2))

    def turned(self, a, way):
        if not self.ring:
            return a
        pairs = a.reshape((self.ring, 2) + a.shape[1:])
        start = (way * (self.me // 2)) % self.ring
        pairs = lax.dynamic_slice_in_dim(
            jnp.concatenate([pairs, pairs]), start, self.ring
        )
        return jnp.where(self.me % 2 == 1, pairs[:, ::-1], pairs).reshape(a.shape)

    def gather(self, arrays):
        if not self.ring:
            gathered = [lax.all_gather(a, "vocab") for a in arrays]
            return [[g[k] for k in range(self.n)] for g in gathered]
        slots = [[None] * self.n for _ in arrays]
        now = list(arrays)
        for step in range(self.ring):
            later = [self.from_ahead(a, 1) for a in now] if step < self.ring - 1 else []
            other = [self.across(a) for a in now]
            for s, a, b in zip(slots, now, other):
                s[2 * step], s[2 * step + 1] = a, b
            if later:
                later, other = lax.optimization_barrier((later, other))
                for s, b in zip(slots, other):
                    s[2 * step + 1] = b
            now = later
        return slots

    def log_sum(self, peak, total):
        def merge(peaks, totals):
            top = functools.reduce(jnp.maximum, peaks)
            return top, sum(t * jnp.exp(p - top) for p, t in zip(peaks, totals))

        both = jnp.stack([peak, total])
        if not self.ring:
            every = lax.all_gather(both, "vocab")
            top = jnp.max(every[:, 0], axis=0)
            return top + jnp.log(jnp.sum(every[:, 1] * jnp.exp(every[:, 0] - top), axis=0))
        every = [both] + [self.from_ahead(both, k) for k in range(1, self.ring)]
        peak, total = merge([e[0] for e in every], [e[1] for e in every])
        both = jnp.stack([peak, total])
        other = self.across(both)
        peak, total = merge([both[0], other[0]], [both[1], other[1]])
        return peak + jnp.log(total)

    def sum_scatter(self, a):
        if not self.ring:
            return lax.psum_scatter(a, "vocab", scatter_dimension=0)
        pairs = a.reshape((self.ring, 2) + a.shape[1:])
        mine = pairs[:, 0] + self.across(pairs[:, 1])
        return mine[0] + sum(self.to_ahead(mine[k], k) for k in range(1, self.ring))


def on_device(teacher_hidden, teacher_gain, teacher_head, student_hidden, student_head, targets):
    f32, bf16, f16 = jnp.float32, jnp.bfloat16, jnp.float16
    teachers = lax.axis_size("teacher")
    t = lax.axis_index("teacher")
    vocab = Vocab()
    nv, v = vocab.n, vocab.me
    weight = 1.0 / teachers
    features, columns = student_head.shape
    block, depth = teacher_hidden.shape[1:]
    piece = block // teachers
    rows = nv * piece

    def sibling(a):
        return lax.ppermute(a, "teacher", [(k, k ^ 1) for k in range(teachers)])

    def facing(a):
        return lax.ppermute(a, "teacher", [(k, k ^ 2) for k in range(teachers)])

    owners = t ^ jnp.array([3, 1, 2, 0], jnp.int32)

    hidden = teacher_hidden[0].astype(f32)
    scale_rows = lax.rsqrt(jnp.mean(hidden * hidden, axis=1, keepdims=True) + EPSILON)
    normed = (hidden * scale_rows * teacher_gain[0][None, :]).astype(bf16)
    normed = normed.reshape(teachers, piece, depth)
    normed = jnp.stack(
        [lax.dynamic_index_in_dim(normed, owners[k], keepdims=False) for k in range(teachers)]
    )

    low = targets % 128
    middle = (targets // 128) % 128
    high = targets // 16384
    digits = jnp.stack([low, middle, high], axis=1).astype(bf16)
    lanes = -features % 128 + 128
    digits = jnp.pad(digits, ((0, 0), (0, lanes - 3)))
    student_block = jnp.concatenate([student_hidden, digits], axis=1)

    normed_slots, student_slots = vocab.gather([normed, student_block])
    x = jnp.stack(normed_slots, axis=1).reshape(teachers * rows, depth)

    students = jnp.stack(student_slots)
    students = jnp.stack([students, sibling(students)])
    students = jnp.concatenate([students, facing(students)])
    token_block = teachers * vocab.holder_of(jnp.arange(nv))[None, :] + owners[:, None]
    where = (t ^ (token_block // nv)) * nv + vocab.slot_of(token_block % nv)
    token = piece * where.reshape(-1)[:, None] + jnp.arange(piece)[None, :]
    moved = token.reshape(-1)[:, None] == jnp.arange(teachers * rows)[None, :]
    students = jnp.dot(
        moved.astype(bf16),
        students.reshape(teachers * rows, -1),
        preferred_element_type=f32,
    )
    students = students.astype(bf16).reshape(teachers, rows, -1)
    h_rows = students[..., :features]
    digits = students[2:, :, features : features + 3].astype(jnp.int32)
    target_rows = digits[..., 0] + 128 * digits[..., 1] + 16384 * digits[..., 2]

    share = features // teachers
    h_share = lax.dynamic_slice_in_dim(h_rows, t * share, share, axis=2)
    h_share = jnp.swapaxes(h_share, 1, 2)

    student_logits = jnp.dot(
        h_rows[2:].reshape(2 * rows, features), student_head, preferred_element_type=f32
    ).reshape(2, rows, columns)

    def by_holder(a):
        return vocab.turned(a.reshape(nv, piece), -1)

    def by_slot(a):
        return vocab.turned(a, 1).reshape(rows)

    near_student = student_logits[1]
    student_peak = jnp.max(near_student, axis=1)
    student_total = jnp.sum(jnp.exp(near_student - student_peak[:, None]), axis=1)
    student_norm = by_slot(vocab.log_sum(by_holder(student_peak), by_holder(student_total)))

    tile, chunks = column_plan(columns, 4)
    near, far, peaks, totals = [], [], [], []
    for first, count in chunks:
        for_sibling, for_own = teacher_chunk(x, teacher_head, weight, tile, first, count)
        from_sibling = sibling(for_sibling)
        to_face = (for_own[:rows] + from_sibling[:rows]).astype(f16)
        kept = (for_own[rows:] + from_sibling[rows:]).astype(f16)
        near_logits = kept.astype(f32) + facing(to_face).astype(f32)
        far_logits = (to_face, facing(kept))
        peak = jnp.max(near_logits, axis=1)
        peaks.append(peak)
        totals.append(jnp.sum(jnp.exp(near_logits - peak[:, None]), axis=1))
        near.append(near_logits)
        far.append(far_logits)

    target_peak = functools.reduce(jnp.maximum, peaks)
    target_total = sum(s * jnp.exp(p - target_peak) for p, s in zip(peaks, totals))
    target_norm = by_slot(vocab.log_sum(by_holder(target_peak), by_holder(target_total)))
    norms = jnp.stack([target_norm, student_norm])
    far_norms = facing(norms)

    def probabilities(mean_logits, logits, norm, wanted, first_column):
        log_target = mean_logits - norm[0][:, None]
        log_student = logits - norm[1][:, None]
        place = v * columns + first_column
        is_target = wanted[:, None] == place + lax.broadcasted_iota(
            jnp.int32, (1, logits.shape[1]), 1
        )
        target_prob = jnp.exp(log_target)
        grad = (
            (1.0 + LABEL_WEIGHT) * jnp.exp(log_student)
            - target_prob
            - LABEL_WEIGHT * is_target.astype(f32)
        ).astype(bf16)
        return log_target, log_student, is_target, target_prob, grad

    losses, hidden_terms, near_grads = [], [], []
    for k, (first, count) in enumerate(chunks):
        a, b = first * tile, (first + count) * tile
        log_target, log_student, is_target, target_prob, grad = probabilities(
            near[k], student_logits[1, :, a:b], norms, target_rows[1], a
        )
        losses.append(
            jnp.sum(target_prob * (log_target - log_student), axis=1)
            - LABEL_WEIGHT * jnp.sum(jnp.where(is_target, log_student, 0.0), axis=1)
        )
        near_grads.append(grad)
        hidden_terms.append(
            lax.dot_general(
                grad, student_head[:, a:b], (((1,), (1,)), ((), ())), preferred_element_type=f32
            )
        )
    own_terms = jnp.concatenate(
        [sum(hidden_terms), jnp.broadcast_to(sum(losses)[:, None], (rows, lanes))], axis=1
    )
    own_sums = vocab.sum_scatter(own_terms.reshape(nv, piece, features + lanes))
    devices = teachers * nv
    own_sums = lax.ppermute(
        own_sums,
        ("teacher", "vocab"),
        [(k, teachers * (k % nv) + k // nv) for k in range(devices)],
    )
    grad_hidden = own_sums[:, :features].astype(bf16)
    row_loss = own_sums[:, features]

    grad_head = None
    for k, (first, count) in enumerate(chunks):
        a, b = first * tile, (first + count) * tile
        far_mean = far[k][0].astype(f32) + far[k][1].astype(f32)
        far_grad = probabilities(
            far_mean, student_logits[0, :, a:b], far_norms, target_rows[0], a
        )[-1]
        g_parts = [sibling(far_grad), sibling(near_grads[k]), far_grad, near_grads[k]]
        grad_head = head_grad_chunk(
            list(h_share), g_parts, grad_head, columns, tile, first, count
        )
    return (row_loss, grad_hidden, grad_head)


def solution(mesh):
    return jax.shard_map(
        on_device,
        mesh=mesh,
        in_specs=(
            P("teacher", "vocab", None),
            P("teacher", None),
            P("teacher", None, "vocab"),
            P(("teacher", "vocab"), None),
            P(None, "vocab"),
            P(("teacher", "vocab")),
        ),
        out_specs=(P(("teacher", "vocab")), P(("teacher", "vocab"), None), P("teacher", "vocab")),
        check_vma=False,
    )
```

```python
import functools

import jax
import jax.numpy as jnp
from jax import lax
from jax.experimental import pallas as pl
from jax.experimental.pallas import tpu as pltpu
from jax.sharding import PartitionSpec as P

EPSILON = 1e-06
LABEL_WEIGHT = 0.5
MIB = 2**20
SMALL_COST = pl.CostEstimate(flops=1, bytes_accessed=1, transcendentals=0)


def column_plan(columns, split):
    tile = next((w for w in (512, 256, 128) if columns % w == 0), columns)
    tiles = columns // tile
    large = 3 * tiles // 8
    if not split or not large:
        return tile, [(0, tiles)], [[0]]
    return tile, [(0, large), (large, large), (2 * large, tiles - 2 * large)], [[0, 1], [2]]


def run_plan(tile, chunks, run):
    chunks = [chunks[c] for c in run]
    first, count = chunks[0]
    wide = tile
    if len(chunks) > 1:
        wide = max(w for w in range(128, 1793, 128) if (tile * count) % w == 0)
    return wide, [(a * tile // wide, b * tile // wide) for a, b in chunks]


def together(tree):
    return lax.optimization_barrier(tree)


def teacher_kernel(weight, slots, *refs):
    x_refs, w_ref, sibling_ref, own_ref = refs[:slots], refs[slots], refs[slots + 1], refs[slots + 2]
    if len(refs) > slots + 3:
        x_ref = refs[-1]
        pieces, rows = x_refs[0].shape[:2]

        @pl.when(pl.program_id(0) == 0)
        def _():
            for p in range(pieces):
                for s in range(slots):
                    at = (p * slots + s) * rows
                    x_ref[at : at + rows, :] = x_refs[s][p]
    else:
        x_ref = x_refs[0]
    sums = jnp.dot(x_ref[...], w_ref[0], preferred_element_type=jnp.float32) * weight
    half = sums.shape[0] // 2
    sibling_ref[...] = sums[:half]
    own_ref[...] = sums[half:]


def teacher_chunk(slots, head, weight, tile, first, count):
    pieces, piece, depth = slots[0].shape
    rows = pieces * piece * len(slots)
    half = rows // 2
    scratch = [pltpu.VMEM((rows, depth), jnp.bfloat16)]
    if piece % 16:
        slots, scratch = [jnp.stack(slots, axis=1).reshape(rows, depth)], []
    return pl.pallas_call(
        functools.partial(teacher_kernel, weight, len(slots)),
        grid=(count,),
        in_specs=[pl.BlockSpec(a.shape, lambda i, a=a: (0,) * a.ndim) for a in slots]
        + [pl.BlockSpec((1, depth, tile), lambda i: (0, 0, i + first))],
        out_specs=[pl.BlockSpec((half, tile), lambda i: (0, i))] * 2,
        out_shape=[jax.ShapeDtypeStruct((half, tile * count), jnp.float32)] * 2,
        scratch_shapes=scratch,
        compiler_params=pltpu.CompilerParams(vmem_limit_bytes=24 * MIB),
        cost_estimate=SMALL_COST,
    )(*slots, head)


def logits_grad_kernel(spans, parts, tile, first, near, *refs):
    mean_refs = refs[: parts * len(spans)]
    h_ref, head_ref, row_ref, grad_ref = refs[len(mean_refs) : len(mean_refs) + 4]
    step = pl.program_id(0)
    if near:
        loss_ref, hidden_ref = refs[len(mean_refs) + 4 :]

        @pl.when(step == 0)
        def _():
            loss_ref[...] = jnp.zeros_like(loss_ref)
            hidden_ref[...] = jnp.zeros_like(hidden_ref)

    def span(means):
        logits = jnp.dot(h_ref[...], head_ref[...], preferred_element_type=jnp.float32)
        at = 0
        for mean_ref in means:
            size = mean_ref.shape[0]
            rows = slice(at, at + size)
            log_target = mean_ref[...] - row_ref[rows, 0:1]
            log_student = logits[rows] - row_ref[rows, 1:2]
            place = (first + step) * tile + lax.broadcasted_iota(jnp.int32, (size, tile), 1)
            is_target = row_ref[rows, 2:3].astype(jnp.int32) == place
            target_prob = jnp.exp(log_target)
            grad = (1.0 + LABEL_WEIGHT) * jnp.exp(log_student) - target_prob
            grad = jnp.where(is_target, grad - LABEL_WEIGHT, grad)
            grad_ref[rows, :] = grad.astype(jnp.bfloat16)
            if near:
                terms = target_prob * (log_target - log_student)
                terms = jnp.where(is_target, terms - LABEL_WEIGHT * log_student, terms)
                loss_ref[rows, :] += jnp.sum(terms, axis=1, keepdims=True)
            at += size

    for k, (start, count) in enumerate(spans):
        pl.when((step >= start) & (step < start + count))(
            functools.partial(span, mean_refs[k * parts : (k + 1) * parts])
        )
    if near:
        hidden_ref[...] += lax.dot_general(
            head_ref[...],
            grad_ref[...],
            (((1,), (1,)), ((), ())),
            preferred_element_type=jnp.float32,
        )


def logits_grad(means, h, head, row_values, near, tile, chunks):
    rows, features = h.shape
    first = chunks[0][0]
    spans = [(start - first, count) for start, count in chunks]
    steps = sum(count for _, count in chunks)
    whole = lambda a: pl.BlockSpec(a.shape, lambda i: (0,) * a.ndim)

    def at_span(start, count):
        return lambda i: (0, jnp.clip(i - start, 0, count - 1))

    out_specs = [pl.BlockSpec((rows, tile), lambda i: (0, i))]
    out_shape = [jax.ShapeDtypeStruct((rows, steps * tile), jnp.bfloat16)]
    if near:
        out_specs += [
            pl.BlockSpec((rows, 1), lambda i: (0, 0)),
            pl.BlockSpec((features, rows), lambda i: (0, 0)),
        ]
        out_shape += [
            jax.ShapeDtypeStruct((rows, 1), jnp.float32),
            jax.ShapeDtypeStruct((features, rows), jnp.float32),
        ]
    return pl.pallas_call(
        functools.partial(logits_grad_kernel, spans, len(means[0]), tile, first, near),
        grid=(steps,),
        in_specs=[
            pl.BlockSpec((m.shape[0], tile), at_span(*span))
            for parts, span in zip(means, spans)
            for m in parts
        ]
        + [whole(h), pl.BlockSpec((features, tile), lambda i: (0, i + first)), whole(row_values)],
        out_specs=out_specs,
        out_shape=out_shape,
        compiler_params=pltpu.CompilerParams(vmem_limit_bytes=48 * MIB),
        cost_estimate=SMALL_COST,
    )(*[m for parts in means for m in parts], h, head, row_values)


def head_grad_kernel(h_ref, a_ref, b_ref, c_ref, d_ref, *refs):
    grads = jnp.concatenate([a_ref[...], b_ref[...], c_ref[...], d_ref[...]], axis=0)
    refs[-1][...] = jnp.dot(h_ref[...], grads, preferred_element_type=jnp.float32)


def head_grad(h, near, far, so_far, columns, tile, chunks):
    features, rows = h.shape
    part = near[0].shape[0]
    first, steps = chunks[0][0], sum(count for _, count in chunks)
    part_spec = pl.BlockSpec((part, tile), lambda i: (0, i))
    in_specs = [pl.BlockSpec((features, rows), lambda i: (0, 0))]
    in_specs += [part_spec] * 4
    operands = [h, far[0], near[0], far[1], near[1]]
    alias = {}
    if so_far is not None:
        alias = {len(operands): 0}
        in_specs.append(pl.BlockSpec(memory_space=pl.ANY))
        operands.append(so_far)
    return pl.pallas_call(
        head_grad_kernel,
        grid=(steps,),
        in_specs=in_specs,
        out_specs=pl.BlockSpec((features, tile), lambda i: (0, i + first)),
        out_shape=jax.ShapeDtypeStruct((features, columns), jnp.float32),
        input_output_aliases=alias,
        compiler_params=pltpu.CompilerParams(vmem_limit_bytes=16 * MIB),
        cost_estimate=SMALL_COST,
    )(*operands)


class Vocab:
    def __init__(self):
        self.n = lax.axis_size("vocab")
        self.me = lax.axis_index("vocab")
        self.ring = self.n // 2 if self.n in (4, 8) else 0

    def from_ahead(self, a, k):
        n = self.ring
        pairs = [(v, 2 * ((v // 2 - k) % n) + v % 2) for v in range(self.n)]
        return lax.ppermute(a, "vocab", pairs)

    def to_ahead(self, a, k):
        n = self.ring
        pairs = [(v, 2 * ((v // 2 + k) % n) + v % 2) for v in range(self.n)]
        return lax.ppermute(a, "vocab", pairs)

    def across(self, a):
        return lax.ppermute(a, "vocab", [(v, v ^ 1) for v in range(self.n)])

    def slot_of(self, v):
        if not self.ring:
            return v
        return 2 * ((v // 2 - self.me // 2) % self.ring) + ((v % 2) ^ (self.me % 2))

    def holder_of(self, slot):
        if not self.ring:
            return slot
        return 2 * ((slot // 2 + self.me // 2) % self.ring) + ((slot % 2) ^ (self.me % 2))

    def turned(self, a, way):
        if not self.ring:
            return a
        pairs = a.reshape((self.ring, 2) + a.shape[1:])
        start = (way * (self.me // 2)) % self.ring
        pairs = lax.dynamic_slice_in_dim(
            jnp.concatenate([pairs, pairs]), start, self.ring
        )
        return jnp.where(self.me % 2 == 1, pairs[:, ::-1], pairs).reshape(a.shape)

    def log_sum(self, peak, total):
        def merge(parts):
            top = functools.reduce(jnp.maximum, [p[0] for p in parts])
            return jnp.stack([top, sum(p[1] * jnp.exp(p[0] - top) for p in parts)])

        if not self.ring:
            every = lax.all_gather(jnp.stack([peak, total]), "vocab")
            merged = merge([every[k] for k in range(self.n)])
        else:
            both = jnp.stack([peak, total])
            merged = merge([both] + [self.from_ahead(both, k) for k in range(1, self.ring)])

        def close(merged):
            if self.ring:
                merged = merge([merged, self.across(merged)])
            return merged[0] + jnp.log(merged[1])

        return merged, close

    def sum_scatter(self, a):
        if not self.ring:
            return [lambda a: lax.psum_scatter(a, "vocab", scatter_dimension=0)]

        def pair(a):
            pairs = a.reshape((self.ring, 2) + a.shape[1:])
            return pairs[:, 0] + self.across(pairs[:, 1])

        def along(a):
            return a[0] + sum(self.to_ahead(a[k], k) for k in range(1, self.ring))

        return [pair, along]


def on_device(teacher_hidden, teacher_gain, teacher_head, student_hidden, student_head, targets):
    f32, bf16, f16 = jnp.float32, jnp.bfloat16, jnp.float16
    teachers = lax.axis_size("teacher")
    t = lax.axis_index("teacher")
    vocab = Vocab()
    nv, v, steps = vocab.n, vocab.me, vocab.ring
    weight = 1.0 / teachers
    features, columns = student_head.shape
    block, depth = teacher_hidden.shape[1:]
    piece = block // teachers
    rows = nv * piece

    def sibling(a):
        return lax.ppermute(a, "teacher", [(k, k ^ 1) for k in range(teachers)])

    def facing(a):
        return lax.ppermute(a, "teacher", [(k, k ^ 2) for k in range(teachers)])

    owners = [t ^ k for k in (3, 1, 2, 0)]

    hidden = teacher_hidden[0].astype(f32)
    scale_rows = lax.rsqrt(jnp.mean(hidden * hidden, axis=1, keepdims=True) + EPSILON)
    normed = (hidden * scale_rows * teacher_gain[0][None, :]).astype(bf16)
    normed = normed.reshape(teachers, piece, depth)
    normed = jnp.stack(
        [lax.dynamic_index_in_dim(normed, owner, keepdims=False) for owner in owners]
    )

    digits = jnp.stack([targets % 128, (targets // 128) % 128, targets // 16384], axis=1)
    lanes = -features % 128 + 128
    digits = jnp.pad(digits.astype(bf16), ((0, 0), (0, lanes - 3)))
    student_block = jnp.concatenate([student_hidden, digits], axis=1)

    tile, chunks, runs = column_plan(columns, steps > 0)
    bounds = [(0, 3), (3, nv)] if steps else [(0, nv)]
    items = [(p, c) for p in range(len(bounds)) for c in range(len(chunks))]

    held = {"slots": [], "sums": {}, "near": {}, "far": {}, "peak": {}, "total": {}}

    def gather_step(step):
        now = held["slots"][2 * step]
        held["slots"].append(vocab.across(now))
        if step < steps - 1:
            held["slots"].append(vocab.from_ahead(now, 1))
        s = held["students"]
        if step == 0:
            s = jnp.stack([s] + [vocab.from_ahead(s, k) for k in range(1, steps)])
        elif step == 1:
            s = jnp.stack([s, vocab.across(s)], axis=1)
            s = s.reshape((nv,) + s.shape[2:])
        elif step == 2:
            s = jnp.stack([s, facing(s)])
        else:
            s = jnp.stack([s, sibling(s)], axis=1)
        held["students"] = s

    def product(p, c):
        a, b = bounds[p]
        held["sums"][p, c] = teacher_chunk(
            held["slots"][a:b], teacher_head, weight, tile, *chunks[c]
        )

    def meet(p, c):
        for_sibling, own = held["sums"][p, c]
        held["sums"][p, c] = (own, sibling(for_sibling))

    def add(p, c):
        own, other = held["sums"][p, c]
        n = own.shape[0] // 2
        held["sums"][p, c] = (
            (own[:n] + other[:n]).astype(f16),
            (own[n:] + other[n:]).astype(f16),
        )

    def cross(p, c, which):
        sums = held["sums"][p, c]
        held["far" if which else "near"][p, c] = (sums[1 - which], facing(sums[which]))

    def arrive(where, p, c):
        own, other = held[where][p, c]
        held[where][p, c] = own.astype(f32) + other.astype(f32)

    def statistics(p, c):
        arrive("near", p, c)
        a = held["near"][p, c]
        held["peak"][p, c] = jnp.max(a, axis=1)
        held["total"][p, c] = jnp.sum(jnp.exp(a - held["peak"][p, c][:, None]), axis=1)

    def by_holder(a):
        return vocab.turned(a.reshape(nv, piece), -1)

    def by_slot(a):
        return vocab.turned(a, 1).reshape(rows)

    def arrange():
        students = held["students"].reshape(teachers * rows, -1)
        token_block = (
            teachers * vocab.holder_of(jnp.arange(nv))[None, :] + jnp.stack(owners)[:, None]
        )
        place = (t ^ (token_block // nv)) * nv + vocab.slot_of(token_block % nv)
        token = piece * place.reshape(-1)[:, None] + jnp.arange(piece)[None, :]
        moved = token.reshape(-1)[:, None] == jnp.arange(teachers * rows)[None, :]
        students = jnp.dot(moved.astype(bf16), students, preferred_element_type=f32).astype(bf16)
        h_rows = students[:, :features]
        digits = students[2 * rows :, features : features + 3].astype(jnp.int32)
        share = features // teachers
        held["wanted"] = (
            digits[:, 0] + 128 * digits[:, 1] + 16384 * digits[:, 2] - v * columns
        ).astype(f32)
        held["share"] = lax.dynamic_slice_in_dim(h_rows, t * share, share, axis=1).T
        held["h"] = (h_rows[2 * rows : 3 * rows], h_rows[3 * rows :])
        logits = jnp.dot(held["h"][1], student_head, preferred_element_type=f32)
        top = jnp.max(logits, axis=1)
        total = jnp.sum(jnp.exp(logits - top[:, None]), axis=1)
        held["student"] = (by_holder(top), by_holder(total))

    if not steps:
        held["slots"] = list(lax.all_gather(normed, "vocab"))
        s = lax.all_gather(student_block, "vocab")
        s = jnp.stack([s, facing(s)])
        held["students"] = jnp.stack([s, sibling(s)], axis=1)
        for item in items:
            product(*item)
            meet(*item)
            add(*item)
            cross(*item, 0)
            cross(*item, 1)
            statistics(*item)
        arrange()
        merged, close_student = vocab.log_sum(*held["student"])
        held["student"] = close_student(merged)
    else:
        held["slots"], held["students"] = [normed], student_block
        gather_step(0)
        held = together(held)
        last = len(items) - 1
        for stage in range(last + 3):
            if stage >= 2:
                add(*items[stage - 2])
            if stage + 1 < steps:
                gather_step(stage + 1)
            if 1 <= stage <= last + 1:
                meet(*items[stage - 1])
            if stage >= 2:
                cross(*items[stage - 2], 0)
                if items[stage - 2][0] == 0:
                    cross(*items[stage - 2], 1)
                if stage == last + 1:
                    cross(*items[len(chunks)], 1)
            if stage <= last:
                product(*items[stage])
            if stage >= 3:
                statistics(*items[stage - 3])
            if stage == last + 1:
                arrange()
            if stage == last + 2:
                held["student"] = close_student(held["student"])
            held = together(held)
            if stage == last + 1:
                held["student"], close_student = vocab.log_sum(*held["student"])

    if steps:
        statistics(*items[-1])
    peak, total = [], []
    for p in range(len(bounds)):
        parts = [held["peak"][p, c] for c in range(len(chunks))]
        top = functools.reduce(jnp.maximum, parts)
        peak.append(top)
        total.append(
            sum(held["total"][p, c] * jnp.exp(a - top) for c, a in enumerate(parts))
        )
    peak, total = jnp.concatenate(peak), jnp.concatenate(total)
    merged, close_target = vocab.log_sum(by_holder(peak), by_holder(total))
    if steps:
        if len(chunks) > 1:
            cross(1, 1, 1)
        held, merged = together((held, merged))
        if len(chunks) > 2:
            cross(1, 2, 1)
    norms = jnp.stack([by_slot(close_target(merged)), by_slot(held["student"])])

    def grads(where, norms, k, run):
        means = [[held[where][p, c] for p in range(len(bounds))] for c in run]
        values = jnp.stack([*norms, held["wanted"][k * rows : (k + 1) * rows]], axis=1)
        return logits_grad(
            means, held["h"][k], student_head, values, where == "near", *run_plan(tile, chunks, run)
        )

    far_norms = facing(norms)
    near_grads, losses, terms = [], 0.0, 0.0
    for run in runs:
        grad, loss, term = grads("near", norms, 1, run)
        near_grads.append(grad)
        losses, terms = losses + loss, terms + term
    terms = jnp.concatenate([terms.T, jnp.broadcast_to(losses, (rows, lanes))], axis=1)
    for p, c in items:
        arrive("far", p, c)
    held, far_norms, near_grads, terms = together((held, far_norms, near_grads, terms))

    sums = terms.reshape(nv, piece, features + lanes)
    hops = vocab.sum_scatter(sums)
    hops += [
        lambda a: lax.ppermute(
            a,
            ("teacher", "vocab"),
            [(k, teachers * (k % nv) + k // nv) for k in range(teachers * nv)],
        )
    ]
    near_others, far_grads, far_others = [], [], []
    for k, run in enumerate(runs):
        near_others.append(sibling(near_grads[k]))
        if far_grads:
            far_others.append(sibling(far_grads[-1]))
        far_grads += grads("far", far_norms, 0, run)
        if len(hops) > 1:
            sums = hops.pop(0)(sums)
        sums, near_others, far_grads, far_others, held = together(
            (sums, near_others, far_grads, far_others, held)
        )
    far_others.append(sibling(far_grads[-1]))
    for hop in hops:
        sums = hop(sums)
    row_loss = sums[:, features]
    grad_hidden = sums[:, :features].astype(bf16)
    grad_head = None
    for k, run in enumerate(runs):
        grad_head = head_grad(
            held["share"],
            [near_others[k], near_grads[k]],
            [far_others[k], far_grads[k]],
            grad_head,
            columns,
            *run_plan(tile, chunks, run),
        )
    return (row_loss, grad_hidden, grad_head)


def solution(mesh):
    return jax.shard_map(
        on_device,
        mesh=mesh,
        in_specs=(
            P("teacher", "vocab", None),
            P("teacher", None),
            P("teacher", None, "vocab"),
            P(("teacher", "vocab"), None),
            P(None, "vocab"),
            P(("teacher", "vocab")),
        ),
        out_specs=(P(("teacher", "vocab")), P(("teacher", "vocab"), None), P("teacher", "vocab")),
        check_vma=False,
    )
```

```python
import functools

import jax
import jax.numpy as jnp
from jax import lax
from jax.experimental import pallas as pl
from jax.experimental.pallas import tpu as pltpu
from jax.sharding import PartitionSpec as P

EPSILON = 1e-06
LABEL_WEIGHT = 0.5
MIB = 2**20
SMALL_COST = pl.CostEstimate(flops=1, bytes_accessed=1, transcendentals=0)


def column_plan(columns, split):
    tile = next((w for w in (512, 256, 128) if columns % w == 0), columns)
    tiles = columns // tile
    large = 3 * tiles // 8
    if not split or not large:
        return tile, [(0, tiles)], [[0]]
    return tile, [(0, large), (large, large), (2 * large, tiles - 2 * large)], [[0, 1], [2]]


def run_plan(tile, chunks, run):
    chunks = [chunks[c] for c in run]
    first, count = chunks[0]
    wide = tile
    if len(chunks) > 1:
        wide = max(w for w in range(128, 1793, 128) if (tile * count) % w == 0)
    return wide, [(a * tile // wide, b * tile // wide) for a, b in chunks]


def together(tree):
    return lax.optimization_barrier(tree)


def teacher_kernel(weight, slots, *refs):
    x_refs, w_ref, sibling_ref, own_ref = refs[:slots], refs[slots], refs[slots + 1], refs[slots + 2]
    if len(refs) > slots + 3:
        x_ref = refs[-1]
        pieces, rows = x_refs[0].shape[:2]

        @pl.when(pl.program_id(0) == 0)
        def _():
            for p in range(pieces):
                for s in range(slots):
                    at = (p * slots + s) * rows
                    x_ref[at : at + rows, :] = x_refs[s][p]
    else:
        x_ref = x_refs[0]
    sums = jnp.dot(x_ref[...], w_ref[0], preferred_element_type=jnp.float32) * weight
    half = sums.shape[0] // 2
    sibling_ref[...] = sums[:half]
    own_ref[...] = sums[half:]


def teacher_chunk(slots, head, weight, tile, first, count):
    pieces, piece = slots[0].shape[:2]
    depth = head.shape[1]
    rows = pieces * piece * len(slots)
    half = rows // 2
    scratch = [pltpu.VMEM((rows, depth), jnp.bfloat16)]
    if piece % 16:
        slots, scratch = [jnp.stack(slots, axis=1).reshape(rows, depth)], []
    return pl.pallas_call(
        functools.partial(teacher_kernel, weight, len(slots)),
        grid=(count,),
        in_specs=[
            pl.BlockSpec(a.shape[:-1] + (depth,), lambda i, a=a: (0,) * a.ndim) for a in slots
        ]
        + [pl.BlockSpec((1, depth, tile), lambda i: (0, 0, i + first))],
        out_specs=[pl.BlockSpec((half, tile), lambda i: (0, i))] * 2,
        out_shape=[jax.ShapeDtypeStruct((half, tile * count), jnp.float32)] * 2,
        scratch_shapes=scratch,
        compiler_params=pltpu.CompilerParams(vmem_limit_bytes=24 * MIB),
        cost_estimate=SMALL_COST,
    )(*slots, head)


def logits_grad_kernel(spans, parts, tile, first, near, *refs):
    mean_refs = refs[: parts * len(spans)]
    h_ref, head_ref, row_ref, grad_ref = refs[len(mean_refs) : len(mean_refs) + 4]
    step = pl.program_id(0)
    if near:
        loss_ref, hidden_ref = refs[len(mean_refs) + 4 :]

        @pl.when(step == 0)
        def _():
            loss_ref[...] = jnp.zeros_like(loss_ref)
            hidden_ref[...] = jnp.zeros_like(hidden_ref)

    def span(means):
        logits = jnp.dot(h_ref[...], head_ref[...], preferred_element_type=jnp.float32)
        at = 0
        for mean_ref in means:
            size = mean_ref.shape[0]
            rows = slice(at, at + size)
            log_target = mean_ref[...] - row_ref[rows, 0:1]
            log_student = logits[rows] - row_ref[rows, 1:2]
            place = (first + step) * tile + lax.broadcasted_iota(jnp.int32, (size, tile), 1)
            is_target = row_ref[rows, 2:3].astype(jnp.int32) == place
            target_prob = jnp.exp(log_target)
            grad = (1.0 + LABEL_WEIGHT) * jnp.exp(log_student) - target_prob
            grad = jnp.where(is_target, grad - LABEL_WEIGHT, grad)
            grad_ref[rows, :] = grad.astype(jnp.bfloat16)
            if near:
                terms = target_prob * (log_target - log_student)
                terms = jnp.where(is_target, terms - LABEL_WEIGHT * log_student, terms)
                loss_ref[rows, :] += jnp.sum(terms, axis=1, keepdims=True)
            at += size

    for k, (start, count) in enumerate(spans):
        pl.when((step >= start) & (step < start + count))(
            functools.partial(span, mean_refs[k * parts : (k + 1) * parts])
        )
    if near:
        hidden_ref[...] += lax.dot_general(
            head_ref[...],
            grad_ref[...],
            (((1,), (1,)), ((), ())),
            preferred_element_type=jnp.float32,
        )


def logits_grad(means, h, head, row_values, near, tile, chunks):
    rows, features = h.shape
    first = chunks[0][0]
    spans = [(start - first, count) for start, count in chunks]
    steps = sum(count for _, count in chunks)
    whole = lambda a: pl.BlockSpec(a.shape, lambda i: (0,) * a.ndim)

    def at_span(start, count):
        return lambda i: (0, jnp.clip(i - start, 0, count - 1))

    out_specs = [pl.BlockSpec((rows, tile), lambda i: (0, i))]
    out_shape = [jax.ShapeDtypeStruct((rows, steps * tile), jnp.bfloat16)]
    if near:
        out_specs += [
            pl.BlockSpec((rows, 1), lambda i: (0, 0)),
            pl.BlockSpec((features, rows), lambda i: (0, 0)),
        ]
        out_shape += [
            jax.ShapeDtypeStruct((rows, 1), jnp.float32),
            jax.ShapeDtypeStruct((features, rows), jnp.float32),
        ]
    return pl.pallas_call(
        functools.partial(logits_grad_kernel, spans, len(means[0]), tile, first, near),
        grid=(steps,),
        in_specs=[
            pl.BlockSpec((m.shape[0], tile), at_span(*span))
            for parts, span in zip(means, spans)
            for m in parts
        ]
        + [whole(h), pl.BlockSpec((features, tile), lambda i: (0, i + first)), whole(row_values)],
        out_specs=out_specs,
        out_shape=out_shape,
        compiler_params=pltpu.CompilerParams(vmem_limit_bytes=40 * MIB),
        cost_estimate=SMALL_COST,
    )(*[m for parts in means for m in parts], h, head, row_values)


def head_grad_kernel(h_ref, a_ref, b_ref, c_ref, d_ref, *refs):
    grads = jnp.concatenate([a_ref[...], b_ref[...], c_ref[...], d_ref[...]], axis=0)
    refs[-1][...] = jnp.dot(h_ref[...], grads, preferred_element_type=jnp.float32)


def head_grad(h, near, far, so_far, columns, tile, chunks):
    features, rows = h.shape
    part = near[0].shape[0]
    first, steps = chunks[0][0], sum(count for _, count in chunks)
    part_spec = pl.BlockSpec((part, tile), lambda i: (0, i))
    in_specs = [pl.BlockSpec((features, rows), lambda i: (0, 0))]
    in_specs += [part_spec] * 4
    operands = [h, far[0], near[0], far[1], near[1]]
    alias = {}
    if so_far is not None:
        alias = {len(operands): 0}
        in_specs.append(pl.BlockSpec(memory_space=pl.ANY))
        operands.append(so_far)
    return pl.pallas_call(
        head_grad_kernel,
        grid=(steps,),
        in_specs=in_specs,
        out_specs=pl.BlockSpec((features, tile), lambda i: (0, i + first)),
        out_shape=jax.ShapeDtypeStruct((features, columns), jnp.float32),
        input_output_aliases=alias,
        compiler_params=pltpu.CompilerParams(vmem_limit_bytes=16 * MIB),
        cost_estimate=SMALL_COST,
    )(*operands)


class Vocab:
    def __init__(self):
        self.n = lax.axis_size("vocab")
        self.me = lax.axis_index("vocab")
        self.ring = self.n // 2 if self.n in (4, 8) else 0

    def from_ahead(self, a, k):
        n = self.ring
        pairs = [(v, 2 * ((v // 2 - k) % n) + v % 2) for v in range(self.n)]
        return lax.ppermute(a, "vocab", pairs)

    def to_ahead(self, a, k):
        n = self.ring
        pairs = [(v, 2 * ((v // 2 + k) % n) + v % 2) for v in range(self.n)]
        return lax.ppermute(a, "vocab", pairs)

    def across(self, a):
        return lax.ppermute(a, "vocab", [(v, v ^ 1) for v in range(self.n)])

    def slot_of(self, v):
        if not self.ring:
            return v
        return 2 * ((v // 2 - self.me // 2) % self.ring) + ((v % 2) ^ (self.me % 2))

    def holder_of(self, slot):
        if not self.ring:
            return slot
        return 2 * ((slot // 2 + self.me // 2) % self.ring) + ((slot % 2) ^ (self.me % 2))

    def turned(self, a, way):
        if not self.ring:
            return a
        pairs = a.reshape((self.ring, 2) + a.shape[1:])
        start = (way * (self.me // 2)) % self.ring
        pairs = lax.dynamic_slice_in_dim(
            jnp.concatenate([pairs, pairs]), start, self.ring
        )
        return jnp.where(self.me % 2 == 1, pairs[:, ::-1], pairs).reshape(a.shape)

    def log_sum(self, peak, total):
        def merge(parts):
            top = functools.reduce(jnp.maximum, [p[0] for p in parts])
            return jnp.stack([top, sum(p[1] * jnp.exp(p[0] - top) for p in parts)])

        if not self.ring:
            every = lax.all_gather(jnp.stack([peak, total]), "vocab")
            merged = merge([every[k] for k in range(self.n)])
        else:
            both = jnp.stack([peak, total])
            merged = merge([both] + [self.from_ahead(both, k) for k in range(1, self.ring)])

        def close(merged):
            if self.ring:
                merged = merge([merged, self.across(merged)])
            return merged[0] + jnp.log(merged[1])

        return merged, close

    def sum_scatter(self, a):
        if not self.ring:
            return [lambda a: lax.psum_scatter(a, "vocab", scatter_dimension=0)]

        def pair(a):
            pairs = a.reshape((self.ring, 2) + a.shape[1:])
            return pairs[:, 0] + self.across(pairs[:, 1])

        def along(a):
            return a[0] + sum(self.to_ahead(a[k], k) for k in range(1, self.ring))

        return [pair, along]


def on_device(teacher_hidden, teacher_gain, teacher_head, student_hidden, student_head, targets):
    f32, bf16, f16 = jnp.float32, jnp.bfloat16, jnp.float16
    teachers = lax.axis_size("teacher")
    t = lax.axis_index("teacher")
    vocab = Vocab()
    nv, v, steps = vocab.n, vocab.me, vocab.ring
    weight = 1.0 / teachers
    features, columns = student_head.shape
    block, depth = teacher_hidden.shape[1:]
    piece = block // teachers
    rows = nv * piece

    def sibling(a):
        return lax.ppermute(a, "teacher", [(k, k ^ 1) for k in range(teachers)])

    def facing(a):
        return lax.ppermute(a, "teacher", [(k, k ^ 2) for k in range(teachers)])

    owners = [t ^ k for k in (3, 1, 2, 0)]

    hidden = teacher_hidden[0].astype(f32)
    scale_rows = lax.rsqrt(jnp.mean(hidden * hidden, axis=1, keepdims=True) + EPSILON)
    normed = (hidden * scale_rows * teacher_gain[0][None, :]).astype(bf16)
    normed = normed.reshape(teachers, piece, depth)
    normed = jnp.stack(
        [lax.dynamic_index_in_dim(normed, owner, keepdims=False) for owner in owners]
    )

    digits = jnp.stack([targets % 128, (targets // 128) % 128, targets // 16384], axis=1)
    lanes = -(features + 128) % (128 * teachers) + 128
    digits = jnp.pad(digits.astype(bf16), ((0, 0), (0, lanes - 3)))
    student_block = jnp.concatenate([student_hidden, digits], axis=1)

    tile, chunks, runs = column_plan(columns, steps > 0)
    bounds = [(0, 3), (3, nv)] if steps else [(0, nv)]
    items = [(p, c) for p in range(len(bounds)) for c in range(len(chunks))]

    held = {"slots": [], "sums": {}, "near": {}, "far": {}, "peak": {}, "total": {}}

    def gather_step(step):
        now = held["slots"][2 * step]
        held["slots"].append(vocab.across(now))
        if step < steps - 1:
            held["slots"].append(vocab.from_ahead(now, 1))

    def spread_students(stage):
        if stage == steps - 1:
            s = jnp.stack([a[..., depth:] for a in held["slots"]])
            s = jnp.swapaxes(s, 1, 2).reshape(nv, piece, -1)
            held["students"] = (s, facing(s))
        elif stage == steps:
            s = jnp.stack(held["students"])
            held["students"] = (s, sibling(s))
        elif stage == steps + 1:
            held["students"] = jnp.stack(held["students"], axis=1)

    def product(p, c):
        a, b = bounds[p]
        held["sums"][p, c] = teacher_chunk(
            held["slots"][a:b], teacher_head, weight, tile, *chunks[c]
        )

    def meet(p, c):
        for_sibling, own = held["sums"][p, c]
        held["sums"][p, c] = (own, sibling(for_sibling))

    def add(p, c):
        own, other = held["sums"][p, c]
        n = own.shape[0] // 2
        if p == 0:
            held["sums"][p, c] = (own + other).astype(f16)
        else:
            held["sums"][p, c] = (
                (own[:n] + other[:n]).astype(f16),
                (own[n:] + other[n:]).astype(f16),
            )

    def cross(p, c, which):
        sums = held["sums"][p, c]
        held["far" if which else "near"][p, c] = (sums[1 - which], facing(sums[which]))

    def cross_both(p, c):
        sums = held["sums"][p, c]
        held["near"][p, c] = held["far"][p, c] = (sums, facing(sums))

    def arrive(where, p, c):
        own, other = held[where][p, c]
        if p == 0:
            n = own.shape[0] // 2
            low, high = slice(0, n), slice(n, 2 * n)
            own, other = (own[high], other[low]) if where == "near" else (own[low], other[high])
        held[where][p, c] = own.astype(f32) + other.astype(f32)

    def statistics(p, c):
        arrive("near", p, c)
        a = held["near"][p, c]
        held["peak"][p, c] = jnp.max(a, axis=1)
        held["total"][p, c] = jnp.sum(jnp.exp(a - held["peak"][p, c][:, None]), axis=1)

    def by_holder(a):
        return vocab.turned(a.reshape(nv, piece), -1)

    def by_slot(a):
        return vocab.turned(a, 1).reshape(rows)

    def arrange():
        students = held["students"].reshape(teachers * rows, -1)
        token_block = (
            teachers * vocab.holder_of(jnp.arange(nv))[None, :] + jnp.stack(owners)[:, None]
        )
        place = (t ^ (token_block // nv)) * nv + vocab.slot_of(token_block % nv)
        token = piece * place.reshape(-1)[:, None] + jnp.arange(piece)[None, :]
        moved = token.reshape(-1)[:, None] == jnp.arange(teachers * rows)[None, :]
        students = jnp.dot(moved.astype(bf16), students, preferred_element_type=f32).astype(bf16)
        h_rows = students[:, :features]
        digits = students[2 * rows :, features : features + 3].astype(jnp.int32)
        share = features // teachers
        held["wanted"] = (
            digits[:, 0] + 128 * digits[:, 1] + 16384 * digits[:, 2] - v * columns
        ).astype(f32)
        held["share"] = lax.dynamic_slice_in_dim(h_rows, t * share, share, axis=1).T
        held["h"] = (h_rows[2 * rows : 3 * rows], h_rows[3 * rows :])
        logits = jnp.dot(held["h"][1], student_head, preferred_element_type=f32)
        top = jnp.max(logits, axis=1)
        total = jnp.sum(jnp.exp(logits - top[:, None]), axis=1)
        held["student"] = (by_holder(top), by_holder(total))

    if not steps:
        held["slots"] = list(lax.all_gather(normed, "vocab"))
        s = lax.all_gather(student_block, "vocab")
        s = jnp.stack([s, facing(s)])
        held["students"] = jnp.stack([s, sibling(s)], axis=1)
        for item in items:
            product(*item)
            meet(*item)
            add(*item)
            cross_both(*item)
            statistics(*item)
        arrange()
    else:
        beside = jnp.swapaxes(student_block.reshape(piece, teachers, -1), 0, 1)
        held["slots"] = [jnp.concatenate([normed, beside], axis=-1)]
        gather_step(0)
        held = together(held)
        last = len(items) - 1
        for stage in range(last + 3):
            if stage >= 2:
                add(*items[stage - 2])
            if stage + 1 < steps:
                gather_step(stage + 1)
            if 1 <= stage <= last + 1:
                meet(*items[stage - 1])
            spread_students(stage)
            if stage >= 2:
                if items[stage - 2][0] == 0:
                    cross_both(*items[stage - 2])
                else:
                    cross(*items[stage - 2], 0)
                if stage == last + 1:
                    cross(*items[len(chunks)], 1)
            if stage <= last:
                product(*items[stage])
            if stage >= 3:
                statistics(*items[stage - 3])
            if stage == last + 1:
                arrange()
            held = together(held)

    ready = []
    if steps:
        statistics(*items[-1])
    peak, total = [], []
    for p in range(len(bounds)):
        parts = [held["peak"][p, c] for c in range(len(chunks))]
        top = functools.reduce(jnp.maximum, parts)
        peak.append(top)
        total.append(
            sum(held["total"][p, c] * jnp.exp(a - top) for c, a in enumerate(parts))
        )
    peak, total = jnp.concatenate(peak), jnp.concatenate(total)
    both = [jnp.stack(pair) for pair in zip((by_holder(peak), by_holder(total)), held["student"])]
    merged, close = vocab.log_sum(*both)
    if steps:
        if len(chunks) > 1:
            cross(1, 1, 1)
        ready = [(p, c) for p, c in items if p == 0 or c == 0]
        for p, c in ready:
            arrive("far", p, c)
        held, merged = together((held, merged))
        if len(chunks) > 2:
            cross(1, 2, 1)
    norms = jnp.stack([by_slot(a) for a in close(merged)])

    def grads(where, norms, k, run):
        means = [[held[where][p, c] for p in range(len(bounds))] for c in run]
        values = jnp.stack([*norms, held["wanted"][k * rows : (k + 1) * rows]], axis=1)
        return logits_grad(
            means, held["h"][k], student_head, values, where == "near", *run_plan(tile, chunks, run)
        )

    far_norms = facing(norms)
    near_grads, losses, terms = [], 0.0, 0.0
    for run in runs:
        grad, loss, term = grads("near", norms, 1, run)
        near_grads.append(grad)
        losses, terms = losses + loss, terms + term
    terms = jnp.concatenate([terms.T, jnp.broadcast_to(losses, (rows, lanes))], axis=1)
    for p, c in items:
        if (p, c) not in ready:
            arrive("far", p, c)
    held, far_norms, near_grads, terms = together((held, far_norms, near_grads, terms))

    sums = terms.reshape(nv, piece, features + lanes)
    hops = vocab.sum_scatter(sums)
    hops += [
        lambda a: lax.ppermute(
            a,
            ("teacher", "vocab"),
            [(k, teachers * (k % nv) + k // nv) for k in range(teachers * nv)],
        )
    ]
    near_others, far_grads, far_others = [], [], []
    for k, run in enumerate(runs):
        near_others.append(sibling(near_grads[k]))
        if far_grads:
            far_others.append(sibling(far_grads[-1]))
        far_grads += grads("far", far_norms, 0, run)
        if len(hops) > 1:
            sums = hops.pop(0)(sums)
        sums, near_others, far_grads, far_others, held = together(
            (sums, near_others, far_grads, far_others, held)
        )
    far_others.append(sibling(far_grads[-1]))
    for hop in hops:
        sums = hop(sums)
    row_loss = sums[:, features]
    grad_hidden = sums[:, :features].astype(bf16)
    grad_head = None
    for k, run in enumerate(runs):
        grad_head = head_grad(
            held["share"],
            [near_others[k], near_grads[k]],
            [far_others[k], far_grads[k]],
            grad_head,
            columns,
            *run_plan(tile, chunks, run),
        )
    return (row_loss, grad_hidden, grad_head)


def solution(mesh):
    return jax.shard_map(
        on_device,
        mesh=mesh,
        in_specs=(
            P("teacher", "vocab", None),
            P("teacher", None),
            P("teacher", None, "vocab"),
            P(("teacher", "vocab"), None),
            P(None, "vocab"),
            P(("teacher", "vocab")),
        ),
        out_specs=(P(("teacher", "vocab")), P(("teacher", "vocab"), None), P("teacher", "vocab")),
        check_vma=False,
    )
```
